32 devices in a mesh: dp: 4 (over y, x), hidden: 8 (over z, core).
Axes of the slice: x: 2, y: 2, z: 4, core: 2. Of those that a mesh axis runs over, the one named last changes fastest.
Arguments:
- activations: bfloat16 [6144, 1024], P('hidden', 'dp'), may hold values from -6 to 6
- cotangent: bfloat16 [6144, 1024], P('hidden', 'dp'), may hold values from -6 to 6
- in_blocks: bfloat16 [3, 1536, 24576], P(None, None, 'hidden'), may hold values from -0.09375 to 0.09375
- out_blocks: bfloat16 [3, 1536, 24576], P(None, None, 'hidden'), may hold values from -0.046875 to 0.046875
- in_left: bfloat16 [6144, 192], P('hidden'), may hold values from -0.078125 to 0.078125
- in_right: bfloat16 [192, 24576], P(None, 'hidden'), may hold values from -0.4375 to 0.4375
- out_left: bfloat16 [24576, 192], P('hidden'), may hold values from -0.0390625 to 0.0390625
- out_right: bfloat16 [6144, 192], P('hidden'), may hold values from -0.4375 to 0.4375
- factor_slots: int32 [2, 3], replicated, may hold values from 0 to 2, each once within a row
Outputs:
- output: bfloat16 [6144, 1024], P('hidden', 'dp')
- grad_input: bfloat16 [6144, 1024], P('hidden', 'dp')
- grad_in_blocks: float32 [3, 1536, 24576], P(None, None, 'hidden')
- grad_out_blocks: float32 [3, 1536, 24576], P(None, None, 'hidden')
- grad_in_left: float32 [6144, 192], P('hidden')
- grad_in_right: float32 [192, 24576], P(None, 'hidden')
- grad_out_left: float32 [24576, 192], P('hidden')
- grad_out_right: float32 [6144, 192], P('hidden')
The draws below stay inside these ranges and needn't reach their ends.
Inputs may be any that keep to these rules, and one draw needn't show every extreme that they name: `factor_slots`: each row names every weight slice once.
All inputs are finite; a program needn't handle non-finite values.
Results may differ from the reference program's by a relative error of at most 0.006.
Values may be sent and summed in bfloat16 or wider, within the bound.
A program may use at most 576 MiB of HBM per device.

```python
import jax
import jax.numpy as jnp

D = 6144
FF = 24576
R = 192
TOKENS = 1024
BD = 1536
BF = 6144
LOG = 2
NF = 3
N_HIDDEN = 8


def block_scale(rng, dims, cuts, smallest, top_value):
    loudness, own = 1.0, jax.random.fold_in(rng, 6)
    for position, blocks in cuts:
        heights = jnp.exp(jax.random.uniform(jax.random.fold_in(own, position), (blocks,), jnp.float32, smallest / len(cuts), top_value / len(cuts)))
        loudness = loudness * jnp.repeat(heights, dims[position] // blocks).reshape([-1 if axis == position else 1 for axis in range(len(dims))])
    return loudness


def scatter_about(rng, dims, deviation, bound, shards=(), kind=jnp.bfloat16):
    entries = deviation * jax.random.normal(rng, dims, jnp.float32)
    if shards:
        entries = entries * block_scale(rng, dims, shards, -0.22, 0.18)
    return jnp.clip(entries, -bound, bound).astype(kind)


def setup_inputs(seed: int = 0) -> dict:
    seeds = jax.random.split(jax.random.key(seed), 10)
    activations = scatter_about(seeds[0], (D, TOKENS), 1.0, 6.0, ((0, 8), (1, 4)))
    cotangent = scatter_about(seeds[1], (D, TOKENS), 1.0, 6.0, ((0, 8), (1, 4)))
    in_blocks = scatter_about(seeds[2], (NF, BD, FF), (NF * BD) ** -0.5, 0.09375, ((2, 8),))
    out_blocks = scatter_about(seeds[3], (NF, BD, FF), (NF * BF) ** -0.5, 0.046875, ((2, 8),))
    in_left = scatter_about(seeds[4], (D, R), D ** -0.5, 0.078125, ((0, 8),))
    in_right = scatter_about(seeds[5], (R, FF), R ** -0.5, 0.4375, ((1, 8),))
    out_left = scatter_about(seeds[6], (FF, R), FF ** -0.5, 0.0390625, ((0, 8),))
    out_right = scatter_about(seeds[7], (D, R), R ** -0.5, 0.4375, ((0, 8),))
    factor_slots = jax.vmap(lambda own: jax.random.permutation(own, NF))(jax.random.split(seeds[8], 2)).reshape((2, NF)).astype(jnp.int32)
    return dict(activations=activations, cotangent=cotangent, in_blocks=in_blocks, out_blocks=out_blocks, in_left=in_left, in_right=in_right, out_left=out_left, out_right=out_right, factor_slots=factor_slots)


def gelu_curve(values):
    return jax.nn.gelu(values, approximate=True)

def partner_table(blocks):
    block_ids = jnp.arange(blocks, dtype=jnp.int32)
    rows = [block_ids]
    for level in range(LOG):
        rows.append(jnp.bitwise_xor(block_ids, jnp.int32(2 ** level)))
    return jnp.stack(rows)

def split_weights(weights, blocks):
    return weights.astype(jnp.float32).reshape(weights.shape[0], weights.shape[1], blocks, -1).transpose(0, 2, 1, 3)

def join_grad(parts):
    return parts.transpose(1, 0, 2).reshape(parts.shape[1], -1)

def reference(activations, cotangent, in_blocks, out_blocks, in_left, in_right, out_left, out_right, factor_slots):
    blocks = N_HIDDEN // 2
    tokens = activations.shape[1]
    partner_rows = partner_table(blocks)
    slots = factor_slots.astype(jnp.int32)
    in_split = activations.astype(jnp.float32).reshape(blocks, -1, tokens)
    cot_split = cotangent.astype(jnp.float32).reshape(blocks, -1, tokens)
    in_weights = split_weights(in_blocks, blocks)
    out_weights = split_weights(out_blocks, blocks)
    lowrank_in = jnp.dot(in_left.T, activations, preferred_element_type=jnp.float32).astype(jnp.bfloat16)
    preact = jnp.dot(in_right.T, lowrank_in, preferred_element_type=jnp.float32).reshape(blocks, -1, tokens)
    for factor in range(NF):
        preact = preact + jnp.einsum('bch,bct->bht', in_weights[slots[0, factor]], in_split[partner_rows[factor]])
    hidden_act, gelu_back = jax.vjp(gelu_curve, preact)
    hidden_act = hidden_act.astype(jnp.bfloat16)
    act_flat = hidden_act.reshape(FF, tokens)
    act_split = hidden_act.astype(jnp.float32)
    lowrank_out = jnp.dot(out_left.T, act_flat, preferred_element_type=jnp.float32).astype(jnp.bfloat16)
    output = jnp.dot(out_right, lowrank_out, preferred_element_type=jnp.float32).reshape(blocks, -1, tokens)
    for factor in range(NF):
        contrib = jnp.einsum('bch,bht->bct', out_weights[slots[1, factor]], act_split)
        output = output + contrib[partner_rows[factor]]
    output = output.reshape(D, tokens).astype(jnp.bfloat16)
    grad_low_out = jnp.dot(out_right.T, cotangent, preferred_element_type=jnp.float32).astype(jnp.bfloat16)
    grad_act = jnp.dot(out_left, grad_low_out, preferred_element_type=jnp.float32).reshape(blocks, -1, tokens)
    out_stack = jnp.zeros(out_blocks.shape, jnp.float32)
    for factor in range(NF):
        partner_cot = cot_split[partner_rows[factor]]
        grad_act = grad_act + jnp.einsum('bch,bct->bht', out_weights[slots[1, factor]], partner_cot)
        out_stack = out_stack.at[slots[1, factor]].set(join_grad(jnp.einsum('bct,bht->bch', partner_cot, act_split)))
    grad_pre = gelu_back(grad_act)[0].astype(jnp.bfloat16)
    pre_split = grad_pre.astype(jnp.float32)
    pre_flat = grad_pre.reshape(FF, tokens)
    grad_low_in = jnp.dot(in_right, pre_flat, preferred_element_type=jnp.float32).astype(jnp.bfloat16)
    grad_input = jnp.dot(in_left, grad_low_in, preferred_element_type=jnp.float32).reshape(blocks, -1, tokens)
    in_stack = jnp.zeros(in_blocks.shape, jnp.float32)
    for factor in range(NF):
        contrib = jnp.einsum('bch,bht->bct', in_weights[slots[0, factor]], pre_split)
        grad_input = grad_input + contrib[partner_rows[factor]]
        in_stack = in_stack.at[slots[0, factor]].set(join_grad(jnp.einsum('bct,bht->bch', in_split[partner_rows[factor]], pre_split)))
    norm_scale = tokens ** (-0.5)
    return (output, grad_input.reshape(D, tokens).astype(jnp.bfloat16), in_stack * norm_scale, out_stack * norm_scale, jnp.dot(activations, grad_low_in.T, preferred_element_type=jnp.float32) * norm_scale, jnp.dot(lowrank_in, pre_flat.T, preferred_element_type=jnp.float32) * norm_scale, jnp.dot(act_flat, grad_low_out.T, preferred_element_type=jnp.float32) * norm_scale, jnp.dot(cotangent, lowrank_out.T, preferred_element_type=jnp.float32) * norm_scale)
```

```python
import jax
import jax.numpy as jnp
from jax import lax
from jax.sharding import PartitionSpec as P


def dots(former, latter, left, right):
    return lax.dot_general(
        former, latter, (((left,), (right,)), ((), ())), preferred_element_type=jnp.float32
    )


def swap(values, bit):
    return lax.ppermute(
        values, "hidden", [(i, i ^ 1 << bit) for i in range(lax.axis_size("hidden"))]
    )


def by_slot(pieces, slots):
    rows = []
    for slot in range(len(pieces)):
        chosen = pieces[-1]
        for level in range(len(pieces) - 1):
            chosen = jnp.where(slots[level] == slot, pieces[level], chosen)
        rows.append(chosen)
    return jnp.stack(rows)


def pick(values, slot, axis=0):
    return lax.dynamic_index_in_dim(values, slot, axis, keepdims=False)


def both_halves(mine, other, is_first, axis):
    first = jnp.where(is_first, mine, other)
    second = jnp.where(is_first, other, mine)
    return jnp.stack([first, second], axis=axis)


def near_parts(own, slots, levels):
    return by_slot([own] + [swap(own, level + 1) for level in range(levels)], slots)


def gather(values):
    return lax.all_gather(values, "dp", axis=0, tiled=False)


def all_tokens(gathered, is_first):
    groups, factors, rows, tokens = gathered.shape
    full = both_halves(gathered, swap(gathered, 0), is_first, 2)
    return full.transpose(1, 2, 3, 0, 4).reshape(factors * 2 * rows, groups * tokens)


def flat_tokens(gathered):
    groups, rows, tokens = gathered.shape
    return gathered.transpose(1, 0, 2).reshape(rows, groups * tokens)


def reduce_blocks(part, slots, half, levels):
    theirs = pick(part, 1 - half, 1).astype(jnp.bfloat16)
    mine = pick(part, half, 1)
    total = mine + swap(theirs, 0).astype(jnp.float32)
    result = pick(total, slots[0])
    for level in range(levels):
        sent = pick(total, slots[level + 1]).astype(jnp.bfloat16)
        result = result + swap(sent, level + 1).astype(jnp.float32)
    return result


def shards(
    activations,
    cotangent,
    in_blocks,
    out_blocks,
    in_left,
    in_right,
    out_left,
    out_right,
    factor_slots,
):
    levels = lax.axis_size("hidden").bit_length() - 2
    factors = levels + 1
    half = lax.axis_index("hidden") % 2
    is_first = half == 0
    in_slots = [factor_slots[0, level] for level in range(factors)]
    out_slots = [factor_slots[1, level] for level in range(factors)]
    rows, tokens = activations.shape
    rank = in_left.shape[1]
    units = in_blocks.shape[2]
    scale = (lax.axis_size("dp") * tokens) ** (-0.5)
    in_flat = in_blocks.reshape(factors * 2 * rows, units)
    out_flat = out_blocks.reshape(factors * 2 * rows, units)

    act_near = near_parts(activations, in_slots, levels)
    cot_near = near_parts(cotangent, out_slots, levels)
    act_full = both_halves(act_near, swap(act_near, 0), is_first, 1)
    act_full = act_full.reshape(factors * 2 * rows, tokens)
    cot_full = both_halves(cot_near, swap(cot_near, 0), is_first, 1)
    cot_full = cot_full.reshape(factors * 2 * rows, tokens)

    low_first = lax.psum(
        jnp.concatenate(
            [dots(in_left, activations, 0, 0), dots(out_right, cotangent, 0, 0)], axis=0
        ),
        "hidden",
    ).astype(jnp.bfloat16)
    lowrank_in, grad_low_out = low_first[:rank], low_first[rank:]

    preact = dots(act_full, in_flat, 0, 0) + dots(lowrank_in, in_right, 0, 0)
    act_float, gelu_back = jax.vjp(lambda v: jax.nn.gelu(v, approximate=True), preact)
    hidden_act = act_float.astype(jnp.bfloat16)
    hidden_all = gather(hidden_act)
    grad_act = dots(cot_full, out_flat, 0, 0) + dots(grad_low_out, out_left, 0, 1)
    grad_pre = gelu_back(grad_act)[0].astype(jnp.bfloat16)
    pre_all = gather(grad_pre)
    cot_near_all = gather(cot_near)
    act_near_all = gather(act_near)
    first_all = flat_tokens(gather(low_first))

    low_last = lax.psum(
        jnp.concatenate(
            [dots(out_left, hidden_act, 0, 1), dots(in_right, grad_pre, 1, 1)], axis=0
        ),
        "hidden",
    ).astype(jnp.bfloat16)
    lowrank_out, grad_low_in = low_last[:rank], low_last[rank:]
    last_all = flat_tokens(gather(low_last))

    out_part = dots(out_flat, hidden_act, 1, 1).reshape(factors, 2, rows, tokens)
    in_part = dots(in_flat, grad_pre, 1, 1).reshape(factors, 2, rows, tokens)
    output = reduce_blocks(out_part, out_slots, half, levels) + dots(out_right, lowrank_out, 1, 0)
    grad_input = reduce_blocks(in_part, in_slots, half, levels) + dots(in_left, grad_low_in, 1, 0)

    hidden_all = hidden_all.reshape(-1, units)
    pre_all = pre_all.reshape(-1, units)
    cot_all = all_tokens(cot_near_all, is_first)
    act_all = all_tokens(act_near_all, is_first)
    grad_out_blocks = (dots(cot_all, hidden_all, 1, 0) * scale).reshape(out_blocks.shape)
    grad_in_blocks = (dots(act_all, pre_all, 1, 0) * scale).reshape(in_blocks.shape)
    own_act = flat_tokens(pick(act_near_all, in_slots[0], 1))
    own_cot = flat_tokens(pick(cot_near_all, out_slots[0], 1))
    return (
        output.astype(jnp.bfloat16),
        grad_input.astype(jnp.bfloat16),
        grad_in_blocks,
        grad_out_blocks,
        dots(own_act, last_all[rank:], 1, 1) * scale,
        dots(first_all[:rank], pre_all, 1, 0) * scale,
        dots(hidden_all, first_all[rank:], 0, 1) * scale,
        dots(own_cot, last_all[:rank], 1, 1) * scale,
    )


def solution(mesh):
    return jax.shard_map(
        shards,
        mesh=mesh,
        in_specs=(
            P("hidden", "dp"),
            P("hidden", "dp"),
            P(None, None, "hidden"),
            P(None, None, "hidden"),
            P("hidden", None),
            P(None, "hidden"),
            P("hidden", None),
            P("hidden", None),
            P(),
        ),
        out_specs=(
            P("hidden", "dp"),
            P("hidden", "dp"),
            P(None, None, "hidden"),
            P(None, None, "hidden"),
            P("hidden", None),
            P(None, "hidden"),
            P("hidden", None),
            P("hidden", None),
        ),
        check_vma=False,
    )
```
